32 devices in a mesh: seq: 4 (over z), pair: 4 (over y, core), dp: 2 (over x).
Axes of the slice: x: 2, y: 2, z: 4, core: 2. Of those that a mesh axis runs over, the one named last changes fastest.
Arguments:
- embed: bfloat16 [2048, 1536], P(('dp', 'seq')), parts along dimension 0, may hold values from -6 to 6
- attn_gain: float32 [1536], replicated, may hold values from 0.5 to 1.5
- w_query: bfloat16 [1536, 1024], P(None, 'pair'), may hold values from -2.5643096 to 2.5643096
- w_key: bfloat16 [1536, 128], replicated, may hold values from -0.104613624 to 0.104613624
- w_value: bfloat16 [1536, 128], replicated, may hold values from -0.15625 to 0.15625
- w_out: bfloat16 [1024, 1536], P('pair'), may hold values from -0.1875 to 0.1875
- pair_map: bfloat16 [128, 64, 128], P(('dp', 'seq'), 'pair'), parts along dimension 0, may hold values from -6 to 6
- w_row: bfloat16 [1536, 128], replicated, may hold values from -0.625 to 0.625
- w_col: bfloat16 [1536, 128], replicated, may hold values from -0.625 to 0.625
- pair_gain: float32 [128], replicated, may hold values from 0.5 to 1.5
- conv_weight: bfloat16 [3, 3, 128, 128], replicated, may hold values from -0.1875 to 0.1875
Outputs:
- block_out: bfloat16 [2048, 1536], P(('dp', 'seq'), 'pair'), parts along dimension 0
- new_pair: bfloat16 [128, 64, 128], P(('dp', 'seq'), 'pair'), parts along dimension 0
The draws below stay inside these ranges and needn't reach their ends.
There are 2 independent parts, one for each index of `dp`. The reference program is written for one: setup_inputs(seed, part) draws one part's arguments, and reference() takes and returns one part's arrays. A program takes and returns all parts, laid end to end along the dimension named above; an argument that names none is the same for every part. Nothing has to cross between parts.
All inputs are finite; a program needn't handle non-finite values.
Results may differ from the reference program's by a relative error of at most 0.014.
Values may be sent and summed in bfloat16 or wider, within the bound.
A program may use at most 64 MiB of HBM per device.

```python
import jax
import jax.numpy as jnp
from jax import lax

D = 1536
HEADS = 8
HEAD_DIM = 128
CHANNELS = 128
POOL = 16
POSITIONS = 1024
BINS = 64


def shared_key(key):
    base = jnp.clip(jax.random.normal(jax.random.fold_in(key, 11), (D, HEAD_DIM), jnp.float32), -4.0, 4.0)
    return base / D ** 0.5


def draw_w_key(key, part):
    return shared_key(key).astype(jnp.bfloat16)


def draw_w_query(key, part):
    noise = jnp.clip(jax.random.normal(jax.random.fold_in(key, 12), (D, HEADS * HEAD_DIM), jnp.float32), -4.0, 4.0) / D ** 0.5
    result = 3.0 * noise
    return result.astype(jnp.bfloat16)


def block_scale(stream_key, extent, pieces, least, largest):
    level, own = 1.0, jax.random.fold_in(stream_key, 6)
    for position, blocks in pieces:
        steps = jnp.exp(jax.random.uniform(jax.random.fold_in(own, position), (blocks,), jnp.float32, least / len(pieces), largest / len(pieces)))
        level = level * jnp.repeat(steps, extent[position] // blocks).reshape([-1 if axis == position else 1 for axis in range(len(extent))])
    return level


def scatter_about(own_key, dims, width, limit, shards=(), held_as=jnp.bfloat16):
    values = jax.random.normal(own_key, dims, jnp.float32) * width
    if len(shards) > 0:
        values = block_scale(own_key, dims, shards, -0.22, 0.18) * values
    return jnp.clip(values, min=-limit, max=limit).astype(held_as)


def setup_inputs(seed: int = 0, part: int = 0) -> dict:
    streams_of = jax.random.split(jax.random.key(seed), 12)
    own_keys = jax.random.split(jax.random.fold_in(streams_of[11], part), 12)
    embed = scatter_about(own_keys[0], (POSITIONS, D), 1.0, 6.0, ((0, 4),))
    attn_gain = jnp.clip(1.0 + 0.1 * jax.random.normal(streams_of[1], (D,), jnp.float32), 0.5, 1.5)
    w_query = draw_w_query(jax.random.fold_in(streams_of[11], 71), part)
    w_key = draw_w_key(jax.random.fold_in(streams_of[11], 71), part)
    w_value = scatter_about(streams_of[4], (D, HEAD_DIM), D ** -0.5, 0.15625)
    w_out = scatter_about(streams_of[5], (HEADS * HEAD_DIM, D), (HEADS * HEAD_DIM) ** -0.5, 0.1875, ((0, 4),))
    pair_map = scatter_about(own_keys[6], (BINS, BINS, CHANNELS), 1.0, 6.0, ((0, 4), (1, 4)))
    w_row = scatter_about(streams_of[7], (D, CHANNELS), (D // POOL) ** -0.5, 0.625)
    w_col = scatter_about(streams_of[8], (D, CHANNELS), (D // POOL) ** -0.5, 0.625)
    pair_gain = jnp.clip(1.0 + 0.1 * jax.random.normal(streams_of[9], (CHANNELS,), jnp.float32), 0.5, 1.5)
    conv_weight = scatter_about(streams_of[10], (3, 3, CHANNELS, CHANNELS), (9 * CHANNELS) ** -0.5, 0.1875)
    return dict(embed=embed, attn_gain=attn_gain, w_query=w_query, w_key=w_key, w_value=w_value, w_out=w_out, pair_map=pair_map, w_row=w_row, w_col=w_col, pair_gain=pair_gain, conv_weight=conv_weight)


def rms_scale(values, gain):
    return values * lax.rsqrt(lax.optimization_barrier(jnp.mean(values * values, axis=-1, keepdims=True)) + 1e-05) * gain

def rotate(tensor, positions):
    half = tensor.shape[-1] // 2
    freq = 10000.0 ** (-jnp.arange(half, dtype=jnp.float32) / half)
    angles = positions[:, None] * freq[None, :]
    cosine = jnp.cos(angles)[:, None, :]
    sine = jnp.sin(angles)[:, None, :]
    first = tensor[..., :half]
    second = tensor[..., half:]
    return jnp.concatenate([first * cosine - second * sine, first * sine + second * cosine], axis=-1)

def reference(embed, attn_gain, w_query, w_key, w_value, w_out, pair_map, w_row, w_col, pair_gain, conv_weight):
    normed = rms_scale(embed.astype(jnp.float32), attn_gain).astype(jnp.bfloat16)
    positions = jnp.arange(POSITIONS).astype(jnp.float32)
    query = jnp.dot(normed, w_query, preferred_element_type=jnp.float32).reshape(POSITIONS, HEADS, HEAD_DIM)
    query = rotate(query, positions).astype(jnp.bfloat16)
    key = jnp.dot(normed, w_key, preferred_element_type=jnp.float32)[:, None, :]
    key = rotate(key, positions)[:, 0, :].astype(jnp.bfloat16)
    value = jnp.dot(normed, w_value, preferred_element_type=jnp.float32).astype(jnp.bfloat16)
    scale = 1.0 / HEAD_DIM ** 0.5

    def one_head(head_query):
        scores = jnp.dot(head_query, key.T, preferred_element_type=jnp.float32) * scale
        top = lax.optimization_barrier(jnp.max(scores, axis=-1, keepdims=True))
        terms = jnp.exp(scores - top)
        total = lax.optimization_barrier(jnp.sum(terms, axis=-1, keepdims=True))
        mixed = jnp.dot(terms.astype(jnp.bfloat16), value, preferred_element_type=jnp.float32)
        return (mixed / total).astype(jnp.bfloat16)
    attended = lax.map(one_head, query.transpose(1, 0, 2))
    attended = attended.transpose(1, 0, 2).reshape(POSITIONS, HEADS * HEAD_DIM)
    block_out = (embed.astype(jnp.float32) + jnp.dot(attended, w_out, preferred_element_type=jnp.float32)).astype(jnp.bfloat16)
    pooled = lax.optimization_barrier(jnp.mean(normed.astype(jnp.float32).reshape(BINS, POOL, D), axis=1)).astype(jnp.bfloat16)
    row_feat = jnp.dot(pooled, w_row, preferred_element_type=jnp.float32).astype(jnp.bfloat16)
    col_feat = jnp.dot(pooled, w_col, preferred_element_type=jnp.float32).astype(jnp.bfloat16)
    updated = pair_map.astype(jnp.float32) + row_feat.astype(jnp.float32)[:, None, :] * col_feat.astype(jnp.float32)[None, :, :]
    pair_normed = rms_scale(updated, pair_gain).astype(jnp.bfloat16)
    convolved = lax.conv_general_dilated(pair_normed[None], conv_weight, (1, 1), 'SAME', dimension_numbers=('NHWC', 'HWIO', 'NHWC'), preferred_element_type=jnp.float32)[0]
    new_pair = (updated + convolved).astype(jnp.bfloat16)
    return (block_out, new_pair)
```

```python
import functools
import math

import jax
import jax.numpy as jnp
import numpy as np
from jax import lax
from jax.experimental import pallas as pl
from jax.experimental.pallas import tpu as pltpu
from jax.sharding import PartitionSpec as P

POOL = 16
EPS = 1e-05
F32 = jnp.float32
BF16 = jnp.bfloat16
MESH = pl.DeviceIdType.MESH


def rope_table(count, size):
    half = size // 2
    freq = 10000.0 ** (-np.arange(half, dtype=np.float64) / half)
    angles = np.arange(count, dtype=np.float64)[:, None] * freq[None, :]
    cosine, sine = np.cos(angles), np.sin(angles)
    return np.concatenate([cosine, cosine, -sine, sine], axis=1).astype(np.float32)


def dot(a, b):
    return jnp.dot(a, b, preferred_element_type=F32)


def kernel(
    n_seq, n_pair,
    embed, attn_gain, w_query, w_key, w_value, w_out, pair_map, w_row, w_col, pair_gain, conv_weight, table,
    block_out, new_pair,
    x_v, gain_v, wqkv, wrc, tab, pm_v, cw, pg_v, nrm, kv, rc, q_v, max_v, sum_v, acc_v, att, wo, res_v,
    hrow, hcol, hcor, colf, colsend, padded, conv_v, out_v, np_v,
    load_s, kv_ss, kv_rs, sib_ss, sib_rs, rc_ss, rc_rs, wo_ss, wo_rs, halo_ss, halo_rs, att_ss, att_rs, out_s,
):
    tokens, width = x_v.shape
    size = kv.shape[2]
    local = q_v.shape[0] // tokens
    rows, cols, chan = pm_v.shape
    bins = rows
    part = res_v.shape[1]
    hw = local * size
    seq, pair = lax.axis_index("seq"), lax.axis_index("pair")
    core = lax.rem(pair, 2)
    sib = pair + 1 - 2 * core

    def seq_of(d):
        return lax.rem(seq + (d + n_seq), n_seq)

    def pair_of(d):
        return lax.rem(pair + (d + n_pair), n_pair)

    loads = {}

    def load(name, src, dst):
        copy = pltpu.make_async_copy(src, dst, load_s.at[len(loads)])
        copy.start()
        loads[name] = copy

    load("x", embed, x_v)
    load("gain", attn_gain, gain_v)
    load("wk", w_key, wqkv.at[:, 0:size])
    load("wv", w_value, wqkv.at[:, size : 2 * size])
    load("tab", table.at[pl.ds(pl.multiple_of(seq * tokens, tokens), tokens)], tab)
    load("wq", w_query, wqkv.at[:, 2 * size : 2 * size + hw])
    load("pm", pair_map, pm_v)
    load("wr", w_row, wrc.at[:, 0:chan])
    load("wc", w_col, wrc.at[:, chan : 2 * chan])
    load("pg", pair_gain, pg_v)
    for i in range(3):
        for j in range(3):
            load(
                ("cw", i, j), conv_weight.at[i, j],
                cw.at[i * chan : (i + 1) * chan, j * chan : (j + 1) * chan],
            )
    mine = pl.ds(pl.multiple_of(pair * part, 128), part)
    load("wo", w_out.at[:, mine], wo.at[pl.ds(pl.multiple_of(pair * hw, 128), hw)])
    load("res", embed.at[:, mine], res_v)

    barrier = pltpu.get_barrier_semaphore()
    count = 0
    for d in range(1, n_seq):
        pl.semaphore_signal(barrier, inc=1, device_id={"seq": seq_of(d)}, device_id_type=MESH)
        count += 1
    for d in range(1, n_pair):
        pl.semaphore_signal(barrier, inc=1, device_id={"pair": pair_of(d)}, device_id_type=MESH)
        count += 1
    for a in (1, -1):
        for b in (1, -1):
            pl.semaphore_signal(
                barrier, inc=1, device_id={"seq": seq_of(a), "pair": pair_of(b)}, device_id_type=MESH
            )
            count += 1

    loads["x"].wait()
    loads["gain"].wait()
    x = x_v[...].astype(F32)
    scale = lax.rsqrt(jnp.mean(x * x, axis=-1, keepdims=True) + EPS)
    nrm[...] = (x * scale * gain_v[...]).astype(BF16)

    pl.semaphore_wait(barrier, count)

    def remote(src, dst, send, recv, **where):
        copy = pltpu.make_async_remote_copy(
            src_ref=src, dst_ref=dst, send_sem=send, recv_sem=recv, device_id=where, device_id_type=MESH
        )
        copy.start()
        return copy

    sent = []
    wo_mine = wo.at[pl.ds(pl.multiple_of(pair * hw, 128), hw)]
    for d in (2, 1, 3) if n_pair == 4 else range(1, n_pair):
        target = pair_of(d)
        sent.append(
            remote(
                w_out.at[:, pl.ds(pl.multiple_of(target * part, 128), part)], wo_mine,
                wo_ss.at[d], wo_rs.at[d], pair=target,
            )
        )

    loads["wk"].wait()
    loads["wv"].wait()
    loads["tab"].wait()
    cc, ss = tab[:, 0:size], tab[:, size : 2 * size]

    def rope(t):
        return t * cc + pltpu.roll(t, size // 2, 1) * ss

    both = dot(nrm[...], wqkv[:, 0 : 2 * size])
    kv[seq, 0:tokens] = rope(both[:, 0:size]).astype(BF16)
    kv[seq, tokens : 2 * tokens] = both[:, size : 2 * size].astype(BF16)
    half = pl.ds(pl.multiple_of(core * tokens, tokens), tokens)

    def offset(i):
        return -((i + 1) // 2) if i % 2 else i // 2

    for i in range(1, n_seq):
        d = -offset(i)
        sent.append(
            remote(
                kv.at[seq, half], kv.at[seq, half], kv_ss.at[i], kv_rs.at[i], seq=seq_of(d)
            )
        )

    loads["pm"].wait()
    for r in range(rows):
        colf[0, r : r + 1] = pm_v[r, cols - 16 : cols].astype(F32)[15:16]
        colf[1, r : r + 1] = pm_v[r, 0:16].astype(F32)[0:1]
    colsend[...] = colf[...].astype(BF16)
    halos = []
    for k, a in enumerate((1, -1)):
        halos.append(
            remote(
                pair_map.at[rows - 1 if a == 1 else 0], hrow.at[k],
                halo_ss.at[k], halo_rs.at[k], seq=seq_of(a),
            )
        )
        halos.append(
            remote(
                colsend.at[k], hcol.at[k], halo_ss.at[2 + k], halo_rs.at[2 + k], pair=pair_of(a)
            )
        )
        for m, b in enumerate((1, -1)):
            slot = 2 * k + m
            halos.append(
                remote(
                    pair_map.at[rows - 1 if a == 1 else 0, pl.ds(cols - 16 if b == 1 else 0, 16)],
                    hcor.at[slot], halo_ss.at[4 + slot], halo_rs.at[4 + slot],
                    seq=seq_of(a), pair=pair_of(b),
                )
            )

    loads["wq"].wait()
    query = dot(nrm[...], wqkv[:, 2 * size : 2 * size + hw])
    for h in range(local):
        q_v[h * tokens : (h + 1) * tokens] = rope(query[:, h * size : (h + 1) * size]).astype(BF16)

    bin_of = lax.broadcasted_iota(jnp.int32, (bins, tokens), 0) * POOL
    at = lax.broadcasted_iota(jnp.int32, (bins, tokens), 1)
    pooler = jnp.where((at >= bin_of) & (at < bin_of + POOL), 1.0 / POOL, 0.0).astype(BF16)
    pooled = dot(pooler, nrm[...]).astype(BF16)
    loads["wr"].wait()
    loads["wc"].wait()
    feats = dot(pooled, wrc[...]).astype(BF16)
    rc[seq, 0:bins] = feats[:, 0:chan]
    rc[seq, bins : 2 * bins] = feats[:, chan : 2 * chan]
    feat_copies = []
    for i in range(1, n_seq):
        feat_copies.append(
            remote(rc.at[seq], rc.at[seq], rc_ss.at[i], rc_rs.at[i], seq=seq_of(-offset(i)))
        )

    factor = math.log2(math.e) / size**0.5
    contract = (((1,), (1,)), ((), ()))

    def attend(b, first):
        scores = lax.dot_general(
            q_v[...], kv[b, 0:tokens], contract, preferred_element_type=F32
        )
        top = jnp.max(scores, axis=-1, keepdims=True)
        if not first:
            old = max_v[...]
            top = jnp.maximum(old, top)
            fix = jnp.exp2((old - top) * factor)
        terms = jnp.exp2((scores - top) * factor)
        total = jnp.sum(terms, axis=-1, keepdims=True)
        mixed = dot(terms.astype(BF16), kv[b, tokens : 2 * tokens])
        max_v[...] = top
        if first:
            sum_v[...] = total
            acc_v[...] = mixed
        else:
            sum_v[...] = sum_v[...] * fix + total
            acc_v[...] = acc_v[...] * fix + mixed

    attend(seq, True)
    forwards = {}

    def receive(i):
        b = seq_of(offset(i))
        pltpu.make_async_remote_copy(
            src_ref=kv.at[b, half], dst_ref=kv.at[b, half], send_sem=kv_ss.at[i], recv_sem=kv_rs.at[i],
            device_id={"seq": b}, device_id_type=MESH,
        ).wait_recv()
        forwards[i] = remote(kv.at[b, half], kv.at[b, half], sib_ss.at[i], sib_rs.at[i], pair=sib)

    for i in range(1, n_seq + 1):
        if i < n_seq:
            receive(i)
        if i > 1:
            forwards[i - 1].wait_recv()
            attend(seq_of(offset(i - 1)), False)

    attended = (acc_v[...] / sum_v[...]).astype(BF16)
    for h in range(local):
        att[pair, :, h * size : (h + 1) * size] = attended[h * tokens : (h + 1) * tokens]

    chips = n_pair // 2
    across = []
    for d in range(1, chips):
        across.append(
            remote(
                att.at[pair], att.at[pair], att_ss.at[d], att_rs.at[d],
                pair=lax.rem(pair + 2 * d, n_pair),
            )
        )
    near = remote(att.at[pair], att.at[pair], att_ss.at[0], att_rs.at[0], pair=sib)

    for copy in halos + feat_copies:
        copy.wait_recv()
    for name in loads:
        if name == "pg" or name[0] == "cw":
            loads[name].wait()
    pg = pg_v[...]

    def normal(u):
        return u * lax.rsqrt(jnp.mean(u * u, axis=-1, keepdims=True) + EPS) * pg

    own = rc[seq].astype(F32)
    row_main = own[0:bins]
    row_low = rc[seq_of(-1)].astype(F32)[bins - 1 : bins]
    row_high = rc[seq_of(1)].astype(F32)[0:1]
    per = cols // bins
    col_main = jnp.concatenate(
        [rc[pair * per + j, bins : 2 * bins].astype(F32) for j in range(per)], axis=0
    )
    col_low = rc[lax.rem(pair * per + (n_seq - 1), n_seq)].astype(F32)[2 * bins - 1 : 2 * bins]
    col_high = rc[lax.rem(pair * per + per, n_seq)].astype(F32)[bins : bins + 1]
    has = [
        jnp.where(seq > 0, 1.0, 0.0), jnp.where(seq < n_seq - 1, 1.0, 0.0),
        jnp.where(pair > 0, 1.0, 0.0), jnp.where(pair < n_pair - 1, 1.0, 0.0),
    ]
    padded[...] = jnp.zeros_like(padded)
    updated = pm_v[...].astype(F32) + row_main[:, None, :] * col_main[None, :, :]
    padded[1 : rows + 1, 8 : 8 + cols] = normal(updated)
    padded[0, 8 : 8 + cols] = normal(hrow[0].astype(F32) + row_low * col_main) * has[0]
    padded[rows + 1, 8 : 8 + cols] = normal(hrow[1].astype(F32) + row_high * col_main) * has[1]
    low = normal(hcol[0].astype(F32) + row_main * col_low) * has[2]
    high = normal(hcol[1].astype(F32) + row_main * col_high) * has[3]
    for r in range(rows):
        padded[1 + r, 7:8] = low[r : r + 1]
        padded[1 + r, 8 + cols : 9 + cols] = high[r : r + 1]
    for k, rf in enumerate((row_low, row_high)):
        for m, cf in enumerate((col_low, col_high)):
            corner = hcor[2 * k + m].astype(F32)
            corner = corner[15:16] if m == 0 else corner[0:1]
            place = 7 if m == 0 else 8 + cols
            padded[0 if k == 0 else rows + 1, place : place + 1] = (
                normal(corner + rf * cf) * (has[k] * has[2 + m])
            )
    wide = padded.shape[1]
    window = jnp.concatenate(
        [padded[i : i + rows].reshape(rows * wide, chan).astype(BF16) for i in range(3)], axis=1
    )
    conv_v[...] = dot(window, cw[...]).reshape(rows, wide, 3 * chan)
    total = updated
    for j in range(3):
        total = total + conv_v[:, 7 + j : 7 + j + cols, j * chan : (j + 1) * chan]
    np_v[...] = total.astype(BF16)
    pair_done = pltpu.make_async_copy(np_v, new_pair, out_s.at[0])
    pair_done.start()

    passed = []
    for d in range(1, chips):
        across[d - 1].wait_recv()
        other = lax.rem(pair + (n_pair - 2 * d), n_pair)
        passed.append(
            remote(att.at[other], att.at[other], att_ss.at[chips + d], att_rs.at[chips + d], pair=sib)
        )
    loads["wo"].wait()
    loads["res"].wait()
    for copy in sent[: n_pair - 1]:
        copy.wait_recv()

    def term(p):
        return dot(att[p], wo[pl.ds(pl.multiple_of(p * hw, 128), hw)])

    result = res_v[...].astype(F32) + term(pair)
    for d in range(1, chips):
        result = result + term(lax.rem(pair + (n_pair - 2 * d), n_pair))
    near.wait_recv()
    result = result + term(sib)
    for d in range(1, chips):
        passed[d - 1].wait_recv()
        result = result + term(lax.rem(sib + (n_pair - 2 * d), n_pair))
    out_v[...] = result.astype(BF16)
    out_done = pltpu.make_async_copy(out_v, block_out, out_s.at[1])
    out_done.start()
    for copy in sent + halos + feat_copies + list(forwards.values()) + across + [near] + passed:
        copy.wait_send()
    pair_done.wait()
    out_done.wait()


def per_device(
    embed, attn_gain, w_query, w_key, w_value, w_out, pair_map, w_row, w_col, pair_gain, conv_weight
):
    n_seq, n_pair = lax.axis_size("seq"), lax.axis_size("pair")
    tokens, width = embed.shape
    size = w_key.shape[1]
    hw = w_query.shape[1]
    local = hw // size
    rows, cols, chan = pair_map.shape
    part = width // n_pair
    bins = tokens // POOL
    wide = cols + 16
    table = jnp.asarray(rope_table(n_seq * tokens, size))
    dma = pltpu.SemaphoreType.DMA
    vmem = pltpu.VMEM
    return pl.pallas_call(
        functools.partial(kernel, n_seq, n_pair),
        out_shape=[
            jax.ShapeDtypeStruct((tokens, part), BF16),
            jax.ShapeDtypeStruct(pair_map.shape, BF16),
        ],
        in_specs=[pl.BlockSpec(memory_space=pl.ANY)] * 12,
        out_specs=[pl.BlockSpec(memory_space=pl.ANY)] * 2,
        scratch_shapes=[
            vmem((tokens, width), BF16),
            vmem((1, width), F32),
            vmem((width, 2 * size + hw), BF16),
            vmem((width, 2 * chan), BF16),
            vmem((tokens, 2 * size), F32),
            vmem((rows, cols, chan), BF16),
            vmem((3 * chan, 3 * chan), BF16),
            vmem((1, chan), F32),
            vmem((tokens, width), BF16),
            vmem((n_seq, 2 * tokens, size), BF16),
            vmem((n_seq, 2 * bins, chan), BF16),
            vmem((local * tokens, size), BF16),
            vmem((local * tokens, 1), F32),
            vmem((local * tokens, 1), F32),
            vmem((local * tokens, size), F32),
            vmem((n_pair, tokens, hw), BF16),
            vmem((n_pair * hw, part), BF16),
            vmem((tokens, part), BF16),
            vmem((2, cols, chan), BF16),
            vmem((2, rows, chan), BF16),
            vmem((4, 16, chan), BF16),
            vmem((2, rows, chan), F32),
            vmem((2, rows, chan), BF16),
            vmem((rows + 2, wide, chan), F32),
            vmem((rows, wide, 3 * chan), F32),
            vmem((tokens, part), BF16),
            vmem((rows, cols, chan), BF16),
            dma((21,)),
            dma((n_seq,)),
            dma((n_seq,)),
            dma((n_seq,)),
            dma((n_seq,)),
            dma((n_seq,)),
            dma((n_seq,)),
            dma((n_pair,)),
            dma((n_pair,)),
            dma((8,)),
            dma((8,)),
            dma((n_pair,)),
            dma((n_pair,)),
            dma((2,)),
        ],
        compiler_params=pltpu.CompilerParams(
            collective_id=0, has_side_effects=True, vmem_limit_bytes=56 * 1024 * 1024
        ),
    )(
        embed, attn_gain.reshape(1, width), w_query, w_key, w_value, w_out, pair_map, w_row, w_col,
        pair_gain.reshape(1, chan), conv_weight, table,
    )


def solution(mesh):
    placed = (
        P(("dp", "seq"), None),
        P(),
        P(None, "pair"),
        P(),
        P(),
        P("pair", None),
        P(("dp", "seq"), "pair", None),
        P(),
        P(),
        P(),
        P(),
    )
    return jax.shard_map(
        per_device,
        mesh=mesh,
        in_specs=placed,
        out_specs=(P(("dp", "seq"), "pair"), P(("dp", "seq"), "pair", None)),
        check_vma=False,
    )
```

```python
import functools
import math

import jax
import jax.numpy as jnp
import numpy as np
from jax import lax
from jax.experimental import pallas as pl
from jax.experimental.pallas import tpu as pltpu
from jax.sharding import PartitionSpec as P

POOL = 16
EPS = 1e-05
F32 = jnp.float32
BF16 = jnp.bfloat16
MESH = pl.DeviceIdType.MESH


def rope_table(count, size):
    half = size // 2
    freq = 10000.0 ** (-np.arange(half, dtype=np.float64) / half)
    angles = np.arange(count, dtype=np.float64)[:, None] * freq[None, :]
    cosine, sine = np.cos(angles), np.sin(angles)
    return np.concatenate([cosine, cosine, -sine, sine], axis=1).astype(np.float32)


def dot(a, b):
    return jnp.dot(a, b, preferred_element_type=F32)


def kernel(
    n_seq, n_pair,
    embed, attn_gain, w_query, w_key, w_value, w_out, pair_map, w_row, w_col, pair_gain, conv_weight, table,
    block_out, new_pair,
    x_v, gain_v, wqkv, wrc, tab, pm_v, cw, pg_v, nrm, kv, rc, q_v, max_v, sum_v, acc_v, att, wo, res_v,
    hrow, hcol, hcor, colf, colsend, padded, conv_v, out_v, np_v,
    load_s, kv_ss, kv_rs, sib_ss, sib_rs, rc_ss, rc_rs, wo_ss, wo_rs, halo_ss, halo_rs, att_ss, att_rs, out_s,
):
    tokens, width = x_v.shape
    size = kv.shape[2]
    local = q_v.shape[0] // tokens
    rows, cols, chan = pm_v.shape
    bins = rows
    part = res_v.shape[1]
    hw = local * size
    seq, pair = lax.axis_index("seq"), lax.axis_index("pair")
    core = lax.rem(pair, 2)
    sib = pair + 1 - 2 * core

    def seq_of(d):
        return lax.rem(seq + (d + n_seq), n_seq)

    def pair_of(d):
        return lax.rem(pair + (d + n_pair), n_pair)

    loads = {}

    def load(name, src, dst):
        copy = pltpu.make_async_copy(src, dst, load_s.at[len(loads)])
        copy.start()
        loads[name] = copy

    load("x", embed, x_v)
    load("gain", attn_gain, gain_v)
    load("wk", w_key, wqkv.at[:, 0:size])
    load("wv", w_value, wqkv.at[:, size : 2 * size])
    load("tab", table.at[pl.ds(pl.multiple_of(seq * tokens, tokens), tokens)], tab)
    load("wq", w_query, wqkv.at[:, 2 * size : 2 * size + hw])
    load("pm", pair_map, pm_v)
    load("wr", w_row, wrc.at[:, 0:chan])
    load("wc", w_col, wrc.at[:, chan : 2 * chan])
    load("pg", pair_gain, pg_v)
    for i in range(3):
        for j in range(3):
            load(
                ("cw", i, j), conv_weight.at[i, j],
                cw.at[i * chan : (i + 1) * chan, j * chan : (j + 1) * chan],
            )
    mine = pl.ds(pl.multiple_of(pair * part, 128), part)
    load("wo", w_out.at[:, mine], wo.at[pl.ds(pl.multiple_of(pair * hw, 128), hw)])
    load("res", embed.at[:, mine], res_v)

    barrier = pltpu.get_barrier_semaphore()
    count = 0
    for d in range(1, n_seq):
        pl.semaphore_signal(barrier, inc=1, device_id={"seq": seq_of(d)}, device_id_type=MESH)
        count += 1
    for d in range(1, n_pair):
        pl.semaphore_signal(barrier, inc=1, device_id={"pair": pair_of(d)}, device_id_type=MESH)
        count += 1
    for a in (1, -1):
        for b in (1, -1):
            pl.semaphore_signal(
                barrier, inc=1, device_id={"seq": seq_of(a), "pair": pair_of(b)}, device_id_type=MESH
            )
            count += 1

    loads["x"].wait()
    loads["gain"].wait()
    x = x_v[...].astype(F32)
    scale = lax.rsqrt(jnp.mean(x * x, axis=-1, keepdims=True) + EPS)
    nrm[...] = (x * scale * gain_v[...][None, :]).astype(BF16)

    pl.semaphore_wait(barrier, count)

    def remote(src, dst, send, recv, **where):
        copy = pltpu.make_async_remote_copy(
            src_ref=src, dst_ref=dst, send_sem=send, recv_sem=recv, device_id=where, device_id_type=MESH
        )
        copy.start()
        return copy

    sent = []
    wo_mine = wo.at[pl.ds(pl.multiple_of(pair * hw, 128), hw)]
    for d in (2, 1, 3) if n_pair == 4 else range(1, n_pair):
        target = pair_of(d)
        sent.append(
            remote(
                w_out.at[:, pl.ds(pl.multiple_of(target * part, 128), part)], wo_mine,
                wo_ss.at[d], wo_rs.at[d], pair=target,
            )
        )

    loads["wk"].wait()
    loads["wv"].wait()
    loads["tab"].wait()
    cc, ss = tab[:, 0:size], tab[:, size : 2 * size]

    def rope(t):
        return t * cc + pltpu.roll(t, size // 2, 1) * ss

    both = dot(nrm[...], wqkv[:, 0 : 2 * size])
    kv[seq, 0:tokens] = rope(both[:, 0:size]).astype(BF16)
    kv[seq, tokens : 2 * tokens] = both[:, size : 2 * size].astype(BF16)
    half = pl.ds(pl.multiple_of(core * tokens, tokens), tokens)

    def offset(i):
        return -((i + 1) // 2) if i % 2 else i // 2

    for i in range(1, n_seq):
        d = -offset(i)
        sent.append(
            remote(
                kv.at[seq, half], kv.at[seq, half], kv_ss.at[i], kv_rs.at[i], seq=seq_of(d)
            )
        )

    loads["pm"].wait()
    for r in range(rows):
        colf[0, r : r + 1] = pm_v[r, cols - 16 : cols].astype(F32)[15:16]
        colf[1, r : r + 1] = pm_v[r, 0:16].astype(F32)[0:1]
    colsend[...] = colf[...].astype(BF16)
    halos = []
    for k, a in enumerate((1, -1)):
        halos.append(
            remote(
                pair_map.at[rows - 1 if a == 1 else 0], hrow.at[k],
                halo_ss.at[k], halo_rs.at[k], seq=seq_of(a),
            )
        )
        halos.append(
            remote(
                colsend.at[k], hcol.at[k], halo_ss.at[2 + k], halo_rs.at[2 + k], pair=pair_of(a)
            )
        )
        for m, b in enumerate((1, -1)):
            slot = 2 * k + m
            halos.append(
                remote(
                    pair_map.at[rows - 1 if a == 1 else 0, pl.ds(cols - 16 if b == 1 else 0, 16)],
                    hcor.at[slot], halo_ss.at[4 + slot], halo_rs.at[4 + slot],
                    seq=seq_of(a), pair=pair_of(b),
                )
            )

    loads["wq"].wait()
    query = dot(nrm[...], wqkv[:, 2 * size : 2 * size + hw])
    for h in range(local):
        q_v[h * tokens : (h + 1) * tokens] = rope(query[:, h * size : (h + 1) * size]).astype(BF16)

    bin_of = lax.broadcasted_iota(jnp.int32, (bins, tokens), 0) * POOL
    at = lax.broadcasted_iota(jnp.int32, (bins, tokens), 1)
    pooler = jnp.where((at >= bin_of) & (at < bin_of + POOL), 1.0 / POOL, 0.0).astype(BF16)
    pooled = dot(pooler, nrm[...]).astype(BF16)
    loads["wr"].wait()
    loads["wc"].wait()
    feats = dot(pooled, wrc[...]).astype(BF16)
    rc[seq, 0:bins] = feats[:, 0:chan]
    rc[seq, bins : 2 * bins] = feats[:, chan : 2 * chan]
    feat_copies = []
    for i in range(1, n_seq):
        feat_copies.append(
            remote(rc.at[seq], rc.at[seq], rc_ss.at[i], rc_rs.at[i], seq=seq_of(-offset(i)))
        )

    factor = math.log2(math.e) / size**0.5
    contract = (((1,), (1,)), ((), ()))

    def attend(b, first):
        scores = lax.dot_general(
            q_v[...], kv[b, 0:tokens], contract, preferred_element_type=F32
        )
        top = jnp.max(scores, axis=-1, keepdims=True)
        if not first:
            old = max_v[...]
            top = jnp.maximum(old, top)
            fix = jnp.exp2((old - top) * factor)
        terms = jnp.exp2((scores - top) * factor)
        total = jnp.sum(terms, axis=-1, keepdims=True)
        mixed = dot(terms.astype(BF16), kv[b, tokens : 2 * tokens])
        max_v[...] = top
        if first:
            sum_v[...] = total
            acc_v[...] = mixed
        else:
            sum_v[...] = sum_v[...] * fix + total
            acc_v[...] = acc_v[...] * fix + mixed

    attend(seq, True)
    forwards = {}

    def receive(i):
        b = seq_of(offset(i))
        pltpu.make_async_remote_copy(
            src_ref=kv.at[b, half], dst_ref=kv.at[b, half], send_sem=kv_ss.at[i], recv_sem=kv_rs.at[i],
            device_id={"seq": b}, device_id_type=MESH,
        ).wait_recv()
        forwards[i] = remote(kv.at[b, half], kv.at[b, half], sib_ss.at[i], sib_rs.at[i], pair=sib)

    for i in range(1, n_seq + 1):
        if i < n_seq:
            receive(i)
        if i > 1:
            forwards[i - 1].wait_recv()
            attend(seq_of(offset(i - 1)), False)

    attended = (acc_v[...] / sum_v[...]).astype(BF16)
    for h in range(local):
        att[pair, :, h * size : (h + 1) * size] = attended[h * tokens : (h + 1) * tokens]

    chips = n_pair // 2
    across = []
    for d in range(1, chips):
        across.append(
            remote(
                att.at[pair], att.at[pair], att_ss.at[d], att_rs.at[d],
                pair=lax.rem(pair + 2 * d, n_pair),
            )
        )
    near = remote(att.at[pair], att.at[pair], att_ss.at[0], att_rs.at[0], pair=sib)

    for copy in halos + feat_copies:
        copy.wait_recv()
    for name in loads:
        if name == "pg" or name[0] == "cw":
            loads[name].wait()
    pg = pg_v[...]

    def normal(u):
        return u * lax.rsqrt(jnp.mean(u * u, axis=-1, keepdims=True) + EPS) * pg

    own = rc[seq].astype(F32)
    row_main = own[0:bins]
    row_low = rc[seq_of(-1)].astype(F32)[bins - 1 : bins]
    row_high = rc[seq_of(1)].astype(F32)[0:1]
    per = cols // bins
    col_main = jnp.concatenate(
        [rc[pair * per + j, bins : 2 * bins].astype(F32) for j in range(per)], axis=0
    )
    col_low = rc[lax.rem(pair * per + (n_seq - 1), n_seq)].astype(F32)[2 * bins - 1 : 2 * bins]
    col_high = rc[lax.rem(pair * per + per, n_seq)].astype(F32)[bins : bins + 1]
    has = [
        jnp.where(seq > 0, 1.0, 0.0), jnp.where(seq < n_seq - 1, 1.0, 0.0),
        jnp.where(pair > 0, 1.0, 0.0), jnp.where(pair < n_pair - 1, 1.0, 0.0),
    ]
    padded[...] = jnp.zeros_like(padded)
    updated = pm_v[...].astype(F32) + row_main[:, None, :] * col_main[None, :, :]
    padded[1 : rows + 1, 8 : 8 + cols] = normal(updated)
    padded[0, 8 : 8 + cols] = normal(hrow[0].astype(F32) + row_low * col_main) * has[0]
    padded[rows + 1, 8 : 8 + cols] = normal(hrow[1].astype(F32) + row_high * col_main) * has[1]
    low = normal(hcol[0].astype(F32) + row_main * col_low) * has[2]
    high = normal(hcol[1].astype(F32) + row_main * col_high) * has[3]
    for r in range(rows):
        padded[1 + r, 7:8] = low[r : r + 1]
        padded[1 + r, 8 + cols : 9 + cols] = high[r : r + 1]
    for k, rf in enumerate((row_low, row_high)):
        for m, cf in enumerate((col_low, col_high)):
            corner = hcor[2 * k + m].astype(F32)
            corner = corner[15:16] if m == 0 else corner[0:1]
            place = 7 if m == 0 else 8 + cols
            padded[0 if k == 0 else rows + 1, place : place + 1] = (
                normal(corner + rf * cf) * (has[k] * has[2 + m])
            )
    wide = padded.shape[1]
    window = jnp.concatenate(
        [padded[i : i + rows].reshape(rows * wide, chan).astype(BF16) for i in range(3)], axis=1
    )
    conv_v[...] = dot(window, cw[...]).reshape(rows, wide, 3 * chan)
    total = updated
    for j in range(3):
        total = total + conv_v[:, 7 + j : 7 + j + cols, j * chan : (j + 1) * chan]
    np_v[...] = total.astype(BF16)
    pair_done = pltpu.make_async_copy(np_v, new_pair, out_s.at[0])
    pair_done.start()

    passed = []
    for d in range(1, chips):
        across[d - 1].wait_recv()
        other = lax.rem(pair + (n_pair - 2 * d), n_pair)
        passed.append(
            remote(att.at[other], att.at[other], att_ss.at[chips + d], att_rs.at[chips + d], pair=sib)
        )
    loads["wo"].wait()
    loads["res"].wait()
    for copy in sent[: n_pair - 1]:
        copy.wait_recv()

    def term(p):
        return dot(att[p], wo[pl.ds(pl.multiple_of(p * hw, 128), hw)])

    result = res_v[...].astype(F32) + term(pair)
    for d in range(1, chips):
        result = result + term(lax.rem(pair + (n_pair - 2 * d), n_pair))
    near.wait_recv()
    result = result + term(sib)
    for d in range(1, chips):
        passed[d - 1].wait_recv()
        result = result + term(lax.rem(sib + (n_pair - 2 * d), n_pair))
    out_v[...] = result.astype(BF16)
    out_done = pltpu.make_async_copy(out_v, block_out, out_s.at[1])
    out_done.start()
    for copy in sent + halos + feat_copies + list(forwards.values()) + across + [near] + passed:
        copy.wait_send()
    pair_done.wait()
    out_done.wait()


def hand_on(a, b, c, d):
    c[...] = a[...]
    d[...] = b[...]


def per_device(
    embed, attn_gain, w_query, w_key, w_value, w_out, pair_map, w_row, w_col, pair_gain, conv_weight
):
    n_seq, n_pair = lax.axis_size("seq"), lax.axis_size("pair")
    tokens, width = embed.shape
    size = w_key.shape[1]
    hw = w_query.shape[1]
    local = hw // size
    rows, cols, chan = pair_map.shape
    part = width // n_pair
    bins = tokens // POOL
    wide = cols + 16
    table = jnp.asarray(rope_table(n_seq * tokens, size))
    dma = pltpu.SemaphoreType.DMA
    vmem = pltpu.VMEM
    outs = pl.pallas_call(
        functools.partial(kernel, n_seq, n_pair),
        out_shape=[
            jax.ShapeDtypeStruct((tokens, part), BF16),
            jax.ShapeDtypeStruct(pair_map.shape, BF16),
        ],
        in_specs=[pl.BlockSpec(memory_space=pl.ANY)] * 12,
        out_specs=[pl.BlockSpec(memory_space=pl.ANY)] * 2,
        scratch_shapes=[
            vmem((tokens, width), BF16),
            vmem((width,), F32),
            vmem((width, 2 * size + hw), BF16),
            vmem((width, 2 * chan), BF16),
            vmem((tokens, 2 * size), F32),
            vmem((rows, cols, chan), BF16),
            vmem((3 * chan, 3 * chan), BF16),
            vmem((1, chan), F32),
            vmem((tokens, width), BF16),
            vmem((n_seq, 2 * tokens, size), BF16),
            vmem((n_seq, 2 * bins, chan), BF16),
            vmem((local * tokens, size), BF16),
            vmem((local * tokens, 1), F32),
            vmem((local * tokens, 1), F32),
            vmem((local * tokens, size), F32),
            vmem((n_pair, tokens, hw), BF16),
            vmem((n_pair * hw, part), BF16),
            vmem((tokens, part), BF16),
            vmem((2, cols, chan), BF16),
            vmem((2, rows, chan), BF16),
            vmem((4, 16, chan), BF16),
            vmem((2, rows, chan), F32),
            vmem((2, rows, chan), BF16),
            vmem((rows + 2, wide, chan), F32),
            vmem((rows, wide, 3 * chan), F32),
            vmem((tokens, part), BF16),
            vmem((rows, cols, chan), BF16),
            dma((21,)),
            dma((n_seq,)),
            dma((n_seq,)),
            dma((n_seq,)),
            dma((n_seq,)),
            dma((n_seq,)),
            dma((n_seq,)),
            dma((n_pair,)),
            dma((n_pair,)),
            dma((8,)),
            dma((8,)),
            dma((n_pair,)),
            dma((n_pair,)),
            dma((2,)),
        ],
        compiler_params=pltpu.CompilerParams(
            collective_id=0, has_side_effects=True, vmem_limit_bytes=56 * 1024 * 1024
        ),
    )(
        embed, attn_gain, w_query, w_key, w_value, w_out, pair_map, w_row, w_col,
        pair_gain.reshape(1, chan), conv_weight, table,
    )
    return pl.pallas_call(
        hand_on,
        out_shape=[jax.ShapeDtypeStruct(o.shape, o.dtype) for o in outs],
        in_specs=[pl.BlockSpec(memory_space=pltpu.VMEM)] * 2,
        out_specs=[pl.BlockSpec(memory_space=pltpu.VMEM)] * 2,
    )(*outs)


def solution(mesh):
    placed = (
        P(("dp", "seq"), None),
        P(),
        P(None, "pair"),
        P(),
        P(),
        P("pair", None),
        P(("dp", "seq"), "pair", None),
        P(),
        P(),
        P(),
        P(),
    )
    return jax.shard_map(
        per_device,
        mesh=mesh,
        in_specs=placed,
        out_specs=(P(("dp", "seq"), "pair"), P(("dp", "seq"), "pair", None)),
        check_vma=False,
    )
```

```python
import functools
import math

import jax
import jax.numpy as jnp
import numpy as np
from jax import lax
from jax.experimental import pallas as pl
from jax.experimental.pallas import tpu as pltpu
from jax.sharding import PartitionSpec as P

POOL = 16
EPS = 1e-05
F32 = jnp.float32
BF16 = jnp.bfloat16
MESH = pl.DeviceIdType.MESH


def rope_table(count, size):
    half = size // 2
    freq = 10000.0 ** (-np.arange(half, dtype=np.float64) / half)
    angles = np.arange(count, dtype=np.float64)[:, None] * freq[None, :]
    cosine, sine = np.cos(angles), np.sin(angles)
    return np.concatenate([cosine, cosine, -sine, sine], axis=1).astype(np.float32)


def dot(a, b):
    return jnp.dot(a, b, preferred_element_type=F32)


def kernel(
    n_seq, n_pair,
    embed, attn_gain, w_query, w_key, w_value, w_out, pair_map, w_row, w_col, pair_gain, conv_weight, table,
    block_out, new_pair,
    x_v, gain_v, wqkv, wrc, tab, pm_v, cw, pg_v, nrm, kv, rc, q_v, max_v, sum_v, acc_v, att, wo, res_v,
    hrow, hcol, hcor, colf, colsend, padded, conv_v, out_v, np_v,
    load_s, kv_ss, kv_rs, sib_ss, sib_rs, rc_ss, rc_rs, wo_ss, wo_rs, halo_ss, halo_rs, att_ss, att_rs, out_s,
):
    tokens, width = x_v.shape
    size = kv.shape[2]
    local = q_v.shape[0] // tokens
    rows, cols, chan = pm_v.shape
    bins = rows
    part = res_v.shape[1]
    hw = local * size
    seq, pair = lax.axis_index("seq"), lax.axis_index("pair")
    core = lax.rem(pair, 2)
    sib = pair + 1 - 2 * core

    def seq_of(d):
        return lax.rem(seq + (d + n_seq), n_seq)

    def pair_of(d):
        return lax.rem(pair + (d + n_pair), n_pair)

    loads = {}

    def load(name, src, dst):
        copy = pltpu.make_async_copy(src, dst, load_s.at[len(loads)])
        copy.start()
        loads[name] = copy

    load("x", embed, x_v)
    load("gain", attn_gain, gain_v)
    load("wk", w_key, wqkv.at[:, 0:size])
    load("wv", w_value, wqkv.at[:, size : 2 * size])
    load("tab", table.at[pl.ds(pl.multiple_of(seq * tokens, tokens), tokens)], tab)
    load("wq", w_query, wqkv.at[:, 2 * size : 2 * size + hw])
    load("pm", pair_map, pm_v)

    barrier = pltpu.get_barrier_semaphore()
    count = 0
    for d in range(1, n_seq):
        pl.semaphore_signal(barrier, inc=1, device_id={"seq": seq_of(d)}, device_id_type=MESH)
        count += 1
    for d in range(1, n_pair):
        pl.semaphore_signal(barrier, inc=1, device_id={"pair": pair_of(d)}, device_id_type=MESH)
        count += 1
    for a in (1, -1):
        for b in (1, -1):
            pl.semaphore_signal(
                barrier, inc=1, device_id={"seq": seq_of(a), "pair": pair_of(b)}, device_id_type=MESH
            )
            count += 1

    loads["x"].wait()
    loads["gain"].wait()
    x = x_v[...].astype(F32)
    scale = lax.rsqrt(jnp.mean(x * x, axis=-1, keepdims=True) + EPS)
    nrm[...] = (x * scale * gain_v[...][None, :]).astype(BF16)

    pl.semaphore_wait(barrier, count)

    def remote(src, dst, send, recv, **where):
        copy = pltpu.make_async_remote_copy(
            src_ref=src, dst_ref=dst, send_sem=send, recv_sem=recv, device_id=where, device_id_type=MESH
        )
        copy.start()
        return copy

    sent = []
    wo_mine = wo.at[pl.ds(pl.multiple_of(pair * hw, 128), hw)]
    for d in (2, 1, 3) if n_pair == 4 else range(1, n_pair):
        target = pair_of(d)
        sent.append(
            remote(
                w_out.at[:, pl.ds(pl.multiple_of(target * part, 128), part)], wo_mine,
                wo_ss.at[d], wo_rs.at[d], pair=target,
            )
        )

    loads["wk"].wait()
    loads["wv"].wait()
    loads["tab"].wait()
    cc, ss = tab[:, 0:size], tab[:, size : 2 * size]

    def rope(t):
        return t * cc + pltpu.roll(t, size // 2, 1) * ss

    both = dot(nrm[...], wqkv[:, 0 : 2 * size])
    kv[seq, 0:tokens] = rope(both[:, 0:size]).astype(BF16)
    kv[seq, tokens : 2 * tokens] = both[:, size : 2 * size].astype(BF16)
    half = pl.ds(pl.multiple_of(core * tokens, tokens), tokens)

    def offset(i):
        return -((i + 1) // 2) if i % 2 else i // 2

    for i in range(1, n_seq):
        d = -offset(i)
        sent.append(
            remote(
                kv.at[seq, half], kv.at[seq, half], kv_ss.at[i], kv_rs.at[i], seq=seq_of(d)
            )
        )

    loads["pm"].wait()
    for r in range(rows):
        colf[0, r : r + 1] = pm_v[r, cols - 16 : cols].astype(F32)[15:16]
        colf[1, r : r + 1] = pm_v[r, 0:16].astype(F32)[0:1]
    colsend[...] = colf[...].astype(BF16)
    halos = []
    for k, a in enumerate((1, -1)):
        halos.append(
            remote(
                pair_map.at[rows - 1 if a == 1 else 0], hrow.at[k],
                halo_ss.at[k], halo_rs.at[k], seq=seq_of(a),
            )
        )
        halos.append(
            remote(
                colsend.at[k], hcol.at[k], halo_ss.at[2 + k], halo_rs.at[2 + k], pair=pair_of(a)
            )
        )
        for m, b in enumerate((1, -1)):
            slot = 2 * k + m
            halos.append(
                remote(
                    pair_map.at[rows - 1 if a == 1 else 0, pl.ds(cols - 16 if b == 1 else 0, 16)],
                    hcor.at[slot], halo_ss.at[4 + slot], halo_rs.at[4 + slot],
                    seq=seq_of(a), pair=pair_of(b),
                )
            )

    load("wr", w_row, wrc.at[:, 0:chan])
    load("wc", w_col, wrc.at[:, chan : 2 * chan])
    load("pg", pair_gain, pg_v)
    for i in range(3):
        for j in range(3):
            load(
                ("cw", i, j), conv_weight.at[i, j],
                cw.at[i * chan : (i + 1) * chan, j * chan : (j + 1) * chan],
            )
    mine = pl.ds(pl.multiple_of(pair * part, 128), part)
    load("wo", w_out.at[:, mine], wo.at[pl.ds(pl.multiple_of(pair * hw, 128), hw)])
    load("res", embed.at[:, mine], res_v)

    loads["wq"].wait()
    query = dot(nrm[...], wqkv[:, 2 * size : 2 * size + hw])
    for h in range(local):
        q_v[h * tokens : (h + 1) * tokens] = rope(query[:, h * size : (h + 1) * size]).astype(BF16)

    bin_of = lax.broadcasted_iota(jnp.int32, (bins, tokens), 0) * POOL
    at = lax.broadcasted_iota(jnp.int32, (bins, tokens), 1)
    pooler = jnp.where((at >= bin_of) & (at < bin_of + POOL), 1.0 / POOL, 0.0).astype(BF16)
    pooled = dot(pooler, nrm[...]).astype(BF16)
    loads["wr"].wait()
    loads["wc"].wait()
    feats = dot(pooled, wrc[...]).astype(BF16)
    rc[seq, 0:bins] = feats[:, 0:chan]
    rc[seq, bins : 2 * bins] = feats[:, chan : 2 * chan]
    feat_copies = []
    for i in range(1, n_seq):
        feat_copies.append(
            remote(rc.at[seq], rc.at[seq], rc_ss.at[i], rc_rs.at[i], seq=seq_of(-offset(i)))
        )

    factor = math.log2(math.e) / size**0.5
    contract = (((1,), (1,)), ((), ()))

    def attend(b, first):
        scores = lax.dot_general(
            q_v[...], kv[b, 0:tokens], contract, preferred_element_type=F32
        )
        top = jnp.max(scores, axis=-1, keepdims=True)
        if not first:
            old = max_v[...]
            top = jnp.maximum(old, top)
            fix = jnp.exp2((old - top) * factor)
        terms = jnp.exp2((scores - top) * factor)
        total = jnp.sum(terms, axis=-1, keepdims=True)
        mixed = dot(terms.astype(BF16), kv[b, tokens : 2 * tokens])
        max_v[...] = top
        if first:
            sum_v[...] = total
            acc_v[...] = mixed
        else:
            sum_v[...] = sum_v[...] * fix + total
            acc_v[...] = acc_v[...] * fix + mixed

    attend(seq, True)
    forwards = {}

    def receive(i):
        b = seq_of(offset(i))
        pltpu.make_async_remote_copy(
            src_ref=kv.at[b, half], dst_ref=kv.at[b, half], send_sem=kv_ss.at[i], recv_sem=kv_rs.at[i],
            device_id={"seq": b}, device_id_type=MESH,
        ).wait_recv()
        forwards[i] = remote(kv.at[b, half], kv.at[b, half], sib_ss.at[i], sib_rs.at[i], pair=sib)

    for i in range(1, n_seq + 1):
        if i < n_seq:
            receive(i)
        if i > 1:
            forwards[i - 1].wait_recv()
            attend(seq_of(offset(i - 1)), False)

    attended = (acc_v[...] / sum_v[...]).astype(BF16)
    for h in range(local):
        att[pair, :, h * size : (h + 1) * size] = attended[h * tokens : (h + 1) * tokens]

    chips = n_pair // 2
    across = []
    for d in range(1, chips):
        for piece in range(2):
            held = att.at[pair, piece * tokens // 2 : (piece + 1) * tokens // 2]
            across.append(
                remote(
                    held, held, att_ss.at[2 * d + piece], att_rs.at[2 * d + piece],
                    pair=lax.rem(pair + 2 * d, n_pair),
                )
            )
    near = remote(att.at[pair], att.at[pair], att_ss.at[0], att_rs.at[0], pair=sib)

    for copy in halos + feat_copies:
        copy.wait_recv()
    for name in loads:
        if name == "pg" or name[0] == "cw":
            loads[name].wait()
    pg = pg_v[...]

    def normal(u):
        return u * lax.rsqrt(jnp.mean(u * u, axis=-1, keepdims=True) + EPS) * pg

    own = rc[seq].astype(F32)
    row_main = own[0:bins]
    row_low = rc[seq_of(-1)].astype(F32)[bins - 1 : bins]
    row_high = rc[seq_of(1)].astype(F32)[0:1]
    per = cols // bins
    col_main = jnp.concatenate(
        [rc[pair * per + j, bins : 2 * bins].astype(F32) for j in range(per)], axis=0
    )
    col_low = rc[lax.rem(pair * per + (n_seq - 1), n_seq)].astype(F32)[2 * bins - 1 : 2 * bins]
    col_high = rc[lax.rem(pair * per + per, n_seq)].astype(F32)[bins : bins + 1]
    has = [
        jnp.where(seq > 0, 1.0, 0.0), jnp.where(seq < n_seq - 1, 1.0, 0.0),
        jnp.where(pair > 0, 1.0, 0.0), jnp.where(pair < n_pair - 1, 1.0, 0.0),
    ]
    padded[...] = jnp.zeros_like(padded)
    updated = pm_v[...].astype(F32) + row_main[:, None, :] * col_main[None, :, :]
    padded[1 : rows + 1, 8 : 8 + cols] = normal(updated)
    padded[0, 8 : 8 + cols] = normal(hrow[0].astype(F32) + row_low * col_main) * has[0]
    padded[rows + 1, 8 : 8 + cols] = normal(hrow[1].astype(F32) + row_high * col_main) * has[1]
    low = normal(hcol[0].astype(F32) + row_main * col_low) * has[2]
    high = normal(hcol[1].astype(F32) + row_main * col_high) * has[3]
    for r in range(rows):
        padded[1 + r, 7:8] = low[r : r + 1]
        padded[1 + r, 8 + cols : 9 + cols] = high[r : r + 1]
    for k, rf in enumerate((row_low, row_high)):
        for m, cf in enumerate((col_low, col_high)):
            corner = hcor[2 * k + m].astype(F32)
            corner = corner[15:16] if m == 0 else corner[0:1]
            place = 7 if m == 0 else 8 + cols
            padded[0 if k == 0 else rows + 1, place : place + 1] = (
                normal(corner + rf * cf) * (has[k] * has[2 + m])
            )
    wide = padded.shape[1]
    window = jnp.concatenate(
        [padded[i : i + rows].reshape(rows * wide, chan).astype(BF16) for i in range(3)], axis=1
    )
    conv_v[...] = dot(window, cw[...]).reshape(rows, wide, 3 * chan)
    total = updated
    for j in range(3):
        total = total + conv_v[:, 7 + j : 7 + j + cols, j * chan : (j + 1) * chan]
    np_v[...] = total.astype(BF16)
    pair_done = pltpu.make_async_copy(np_v, new_pair, out_s.at[0])
    pair_done.start()

    passed = []
    for d in range(1, chips):
        other = lax.rem(pair + (n_pair - 2 * d), n_pair)
        for piece in range(2):
            across[2 * d - 2 + piece].wait_recv()
            held = att.at[other, piece * tokens // 2 : (piece + 1) * tokens // 2]
            slot = 2 * (chips + d) + piece
            passed.append(remote(held, held, att_ss.at[slot], att_rs.at[slot], pair=sib))
    loads["wo"].wait()
    loads["res"].wait()
    for copy in sent[: n_pair - 1]:
        copy.wait_recv()

    def term(p):
        return dot(att[p], wo[pl.ds(pl.multiple_of(p * hw, 128), hw)])

    result = res_v[...].astype(F32) + term(pair)
    for d in range(1, chips):
        result = result + term(lax.rem(pair + (n_pair - 2 * d), n_pair))
    near.wait_recv()
    result = result + term(sib)
    for d in range(1, chips):
        passed[2 * d - 2].wait_recv()
        passed[2 * d - 1].wait_recv()
        result = result + term(lax.rem(sib + (n_pair - 2 * d), n_pair))
    out_v[...] = result.astype(BF16)
    out_done = pltpu.make_async_copy(out_v, block_out, out_s.at[1])
    out_done.start()
    for copy in sent + halos + feat_copies + list(forwards.values()) + across + [near] + passed:
        copy.wait_send()
    pair_done.wait()
    out_done.wait()


def hand_on(a, b, c, d):
    c[...] = a[...]
    d[...] = b[...]


def per_device(
    embed, attn_gain, w_query, w_key, w_value, w_out, pair_map, w_row, w_col, pair_gain, conv_weight
):
    n_seq, n_pair = lax.axis_size("seq"), lax.axis_size("pair")
    tokens, width = embed.shape
    size = w_key.shape[1]
    hw = w_query.shape[1]
    local = hw // size
    rows, cols, chan = pair_map.shape
    part = width // n_pair
    bins = tokens // POOL
    wide = cols + 16
    table = jnp.asarray(rope_table(n_seq * tokens, size))
    dma = pltpu.SemaphoreType.DMA
    vmem = pltpu.VMEM
    outs = pl.pallas_call(
        functools.partial(kernel, n_seq, n_pair),
        out_shape=[
            jax.ShapeDtypeStruct((tokens, part), BF16),
            jax.ShapeDtypeStruct(pair_map.shape, BF16),
        ],
        in_specs=[pl.BlockSpec(memory_space=pl.ANY)] * 12,
        out_specs=[pl.BlockSpec(memory_space=pl.ANY)] * 2,
        scratch_shapes=[
            vmem((tokens, width), BF16),
            vmem((width,), F32),
            vmem((width, 2 * size + hw), BF16),
            vmem((width, 2 * chan), BF16),
            vmem((tokens, 2 * size), F32),
            vmem((rows, cols, chan), BF16),
            vmem((3 * chan, 3 * chan), BF16),
            vmem((1, chan), F32),
            vmem((tokens, width), BF16),
            vmem((n_seq, 2 * tokens, size), BF16),
            vmem((n_seq, 2 * bins, chan), BF16),
            vmem((local * tokens, size), BF16),
            vmem((local * tokens, 1), F32),
            vmem((local * tokens, 1), F32),
            vmem((local * tokens, size), F32),
            vmem((n_pair, tokens, hw), BF16),
            vmem((n_pair * hw, part), BF16),
            vmem((tokens, part), BF16),
            vmem((2, cols, chan), BF16),
            vmem((2, rows, chan), BF16),
            vmem((4, 16, chan), BF16),
            vmem((2, rows, chan), F32),
            vmem((2, rows, chan), BF16),
            vmem((rows + 2, wide, chan), F32),
            vmem((rows, wide, 3 * chan), F32),
            vmem((tokens, part), BF16),
            vmem((rows, cols, chan), BF16),
            dma((21,)),
            dma((n_seq,)),
            dma((n_seq,)),
            dma((n_seq,)),
            dma((n_seq,)),
            dma((n_seq,)),
            dma((n_seq,)),
            dma((n_pair,)),
            dma((n_pair,)),
            dma((8,)),
            dma((8,)),
            dma((2 * n_pair,)),
            dma((2 * n_pair,)),
            dma((2,)),
        ],
        compiler_params=pltpu.CompilerParams(
            collective_id=0, has_side_effects=True, vmem_limit_bytes=56 * 1024 * 1024
        ),
    )(
        embed, attn_gain, w_query, w_key, w_value, w_out, pair_map, w_row, w_col,
        pair_gain.reshape(1, chan), conv_weight, table,
    )
    return pl.pallas_call(
        hand_on,
        out_shape=[jax.ShapeDtypeStruct(o.shape, o.dtype) for o in outs],
        in_specs=[pl.BlockSpec(memory_space=pltpu.VMEM)] * 2,
        out_specs=[pl.BlockSpec(memory_space=pltpu.VMEM)] * 2,
    )(*outs)


def solution(mesh):
    placed = (
        P(("dp", "seq"), None),
        P(),
        P(None, "pair"),
        P(),
        P(),
        P("pair", None),
        P(("dp", "seq"), "pair", None),
        P(),
        P(),
        P(),
        P(),
    )
    return jax.shard_map(
        per_device,
        mesh=mesh,
        in_specs=placed,
        out_specs=(P(("dp", "seq"), "pair"), P(("dp", "seq"), "pair", None)),
        check_vma=False,
    )
```
